256 devices in a mesh: dp: 64 (over y, z, x_lo), mp: 4 (over x_hi, core).
Axes of the slice: x: 4 (x_hi: 2, x_lo: 2; x = x_hi * 2 + x_lo), y: 4, z: 8, core: 2. Of those that a mesh axis runs over, the one named last changes fastest.
Arguments:
- photo_embedding_matrix: float32 [98304, 1152], P(('dp', 'mp')), may hold values from -1.8 to 1.8
- caption_embedding_matrix: float32 [98304, 1152], P(('dp', 'mp')), may hold values from -1.8 to 1.8
- caption_mate_entry: int32 [98304], P(('dp', 'mp')), may hold values from 0 to 98303, as said below
- sharpness_factor: float32 [1], replicated, may hold values from 0.5 to 2
- affinity_offset: float32 [1], replicated, may hold values from -1 to 1
Outputs:
- grad_images: float32 [98304, 1152], P(('dp', 'mp'))
- text_gradient: float32 [98304, 1152], P(('dp', 'mp'))
The draws below stay inside these ranges and needn't reach their ends.
Inputs may be any that keep to these rules, and one draw needn't show every extreme that they name: `caption_mate_entry`: partner of row i lies in the same aligned block of 384 rows as i, and within each block the partners are a permutation of that block's rows.
All inputs are finite; a program needn't handle non-finite values.
Results may differ from the reference program's by a relative error of at most 0.0001.
Values sent between devices are 32-bit elements; how exact they have to be, the bound alone decides.
A program may use at most 64 MiB of HBM per device.

```python
import math
import jax
import jax.numpy as jnp
from jax import lax

D = 1152
ROWS = 384
HOPS = 4
BATCH = 98304


def draw_caption_mate_entry(key, part):
    key = jax.random.fold_in(key, 11)
    nblocks = BATCH // ROWS
    keys = jax.random.split(key, nblocks)
    perms = jax.vmap(lambda k: jax.random.permutation(k, ROWS))(keys).astype(jnp.int32)
    starts = jnp.arange(nblocks, dtype=jnp.int32)[:, None] * ROWS
    return (perms + starts).reshape(BATCH)


def levels(rng, extent, cuts, low, top_value):
    def one(axis_at, blocks):
        heights = jax.random.uniform(jax.random.fold_in(jax.random.fold_in(rng, 6), axis_at), (blocks,), jnp.float32, low / len(cuts), top_value / len(cuts))
        return jnp.repeat(jnp.exp(heights), extent[axis_at] // blocks).reshape((-1,) + (1,) * (len(extent) - axis_at - 1))

    factor_of = one(*cuts[0])
    for cut in cuts[1:]:
        factor_of = factor_of * one(*cut)
    return factor_of


def scatter_about(stream_key, dims, spread, limit, cuts=(), held_as=jnp.bfloat16):
    factor_of = levels(stream_key, dims, cuts, -0.22, 0.18) if cuts else 1.0
    array = jax.random.normal(stream_key, dims, jnp.float32) * spread * factor_of
    return jnp.minimum(jnp.maximum(array, -limit), limit).astype(held_as)


def setup_inputs(seed: int = 0) -> dict:
    seeds = jax.random.split(jax.random.key(seed), 6)
    return {
        "photo_embedding_matrix": scatter_about(seeds[0], (BATCH, D), 0.3, 1.8, ((0, 256),), jnp.float32),
        "caption_embedding_matrix": scatter_about(seeds[1], (BATCH, D), 0.3, 1.8, ((0, 256),), jnp.float32),
        "caption_mate_entry": draw_caption_mate_entry(jax.random.fold_in(seeds[5], 71), 0),
        "sharpness_factor": jnp.clip(jnp.exp(jax.random.uniform(seeds[3], (1,), jnp.float32, math.log(0.5), math.log(2.0))), 0.5, 2.0),
        "affinity_offset": jnp.clip(jax.random.uniform(seeds[4], (1,), jnp.float32, -1.0, 1.0), -1.0, 1.0),
    }


def reference(photo_embedding_matrix, caption_embedding_matrix, caption_mate_entry, sharpness_factor, affinity_offset):
    nblocks = BATCH // ROWS
    similarity_multiplier = sharpness_factor[0]
    offset = affinity_offset[0]
    picture_block_list = photo_embedding_matrix.reshape(nblocks, ROWS, D)
    text_blocks = caption_embedding_matrix.reshape(nblocks, ROWS, D)
    paired_piece_sequence = caption_mate_entry.reshape(nblocks, ROWS)
    block_ids = jnp.arange(nblocks, dtype=jnp.int32)
    columns = jnp.arange(ROWS, dtype=jnp.int32)
    grad_img = jnp.zeros((nblocks, ROWS, D), jnp.float32)
    grad_txt = jnp.zeros((nblocks, ROWS, D), jnp.float32)
    for hop in range(HOPS + 1):
        arriving_caption_piece = jnp.roll(text_blocks, hop, axis=0)
        owners = (block_ids - hop) % nblocks
        global_column_indices = owners[:, None] * ROWS + columns[None, :]
        scores = jnp.einsum("bid,bjd->bij", picture_block_list, arriving_caption_piece, precision=lax.Precision.HIGHEST)
        logits = similarity_multiplier * scores + offset
        sign = jnp.where(paired_piece_sequence[:, :, None] == global_column_indices[:, None, :], jnp.float32(1.0), jnp.float32(-1.0))
        coef = -sign * jax.nn.sigmoid(-sign * logits) * jnp.float32(1.0 / (HOPS + 1))
        grad_img = grad_img + similarity_multiplier * jnp.einsum("bij,bjd->bid", coef, arriving_caption_piece, precision=lax.Precision.HIGHEST)
        contrib = similarity_multiplier * jnp.einsum("bij,bid->bjd", coef, picture_block_list, precision=lax.Precision.HIGHEST)
        grad_txt = grad_txt + jnp.roll(contrib, -hop, axis=0)
    return grad_img.reshape(BATCH, D), grad_txt.reshape(BATCH, D)
```

```python
import functools

import jax
import jax.numpy as jnp
from jax import lax
from jax.experimental import pallas as pl
from jax.experimental.pallas import tpu as pltpu
from jax.sharding import PartitionSpec as P

HOPS = 4
PIECES = 12
PARTS = 3
PER = PIECES // PARTS
AHEAD = 3
LAG = 1
TEXT, IMAGE, SIB, A2, A4, B2, B4, A2S, B2S, X4S, PASS_P, PASS_Q = range(12)
SLOTS = 12
NT = (((1,), (1,)), ((), ()))


def split(value):
    high = value.astype(jnp.bfloat16)
    return high, (value - high.astype(jnp.float32)).astype(jnp.bfloat16)


def dot(left, right):
    return jnp.dot(left, right, preferred_element_type=jnp.float32)


def dot_nt(left, right):
    return lax.dot_general(left, right, NT, preferred_element_type=jnp.float32)


def kernel(
    planes, text_ref, image_ref, mate_ref, scale_ref, offset_ref, out_ref,
    buf, high_ref, low_ref, send_sem, recv_sem, load_sem,
):
    rows = text_ref.shape[0]
    piece, part = rows // PIECES, rows // PARTS
    dp, mp = lax.axis_index("dp"), lax.axis_index("mp")
    plane, x_lo = dp // 2, dp % 2
    side, core = mp // 2, mp % 2
    outer = jnp.where(x_lo == side, 1, 0)
    is_outer = x_lo == side
    near, far = side, 1 - side
    type_a2 = jnp.where(is_outer, far, near)
    type_b2 = jnp.where(is_outer, near, far)

    def at(z, lo, hi, c):
        return (z * 2 + lo, hi * 2 + c)

    beside = at(plane, 1 - x_lo, side, core)
    across = at(plane, 1 - x_lo, 1 - side, core)
    sibling = at(plane, x_lo, side, 1 - core)
    up = at((plane + 1) % planes, x_lo, side, core)
    down = at((plane + planes - 1) % planes, x_lo, side, core)

    def pick(flag, yes, no):
        return tuple(jnp.where(flag, a, b) for a, b in zip(yes, no))

    z_near = pick(side == 0, up, down)
    z_far = pick(side == 0, down, up)

    def move(flow, source, target, index, device):
        lines = pl.ds(pl.multiple_of(index * piece, piece), piece)
        return pltpu.make_async_remote_copy(
            src_ref=buf.at[source, lines],
            dst_ref=buf.at[target, lines],
            send_sem=send_sem.at[flow, index],
            recv_sem=recv_sem.at[target, index],
            device_id=device,
            device_id_type=pl.DeviceIdType.MESH,
        )

    def arrived(slot, index):
        move(0, slot, slot, index, sibling).wait_recv()

    first_target = jnp.where(is_outer, A4, PASS_P)
    second_target = jnp.where(is_outer, PASS_Q, A2)
    second_device = pick(is_outer, z_far, across)
    third_source = jnp.where(is_outer, PASS_Q, A4)
    fourth_source = jnp.where(is_outer, PASS_Q, far)

    flows = [
        lambda i: move(0, near, first_target, i, beside),
        lambda i: move(1, far, second_target, i, second_device),
        lambda i: move(2, PASS_P, A2, i, across),
        lambda i: move(3, PASS_P, A4, i, z_near),
        lambda i: move(4, third_source, B2, i, across),
        lambda i: move(5, fourth_source, B4, i, beside),
        lambda i: move(6, core, SIB, i, sibling),
        lambda i: move(7, A2, A2S, i, sibling),
        lambda i: move(8, B2, B2S, i, sibling),
        lambda i: move(9, jnp.where(core == side, B4, A4), X4S, i, sibling),
    ]

    load_text = pltpu.make_async_copy(text_ref, buf.at[TEXT], load_sem.at[0])
    load_image = pltpu.make_async_copy(image_ref, buf.at[IMAGE], load_sem.at[1])
    load_text.start()
    load_image.start()

    barrier = pltpu.get_barrier_semaphore()

    def greet(device):
        pl.semaphore_signal(barrier, inc=1, device_id=device, device_id_type=pl.DeviceIdType.MESH)

    for device in (beside, across, sibling):
        greet(device)

    @pl.when(is_outer)
    def _():
        greet(up)
        greet(down)

    load_text.wait()
    load_image.wait()
    pl.semaphore_wait(barrier, 3 + 2 * outer)

    def issue(step):
        @pl.when(step < PIECES)
        def _():
            flows[0](step).start()
            flows[1](step).start()
            flows[6](step).start()

        @pl.when((step >= PIECES) & (step < 2 * PIECES))
        def _():
            index = step - PIECES

            @pl.when(is_outer)
            def _():
                arrived(PASS_Q, index)

            flows[4](index).start()
            flows[5](index).start()

    lax.fori_loop(0, AHEAD, lambda i, c: (issue(i), c)[1], 0)

    scale = scale_ref[0]
    offset = offset_ref[0]
    share = scale * jnp.float32(1.0 / (HOPS + 1))

    for kind, slot in ((0, IMAGE), (1, TEXT)):
        high, low = split(buf[slot])
        high_ref[kind] = high
        low_ref[kind] = low
    logits = dot_nt(high_ref[1], high_ref[0])
    logits += dot_nt(high_ref[1], low_ref[0])
    logits += dot_nt(low_ref[1], high_ref[0])
    mine = (dp * 4 + mp) * rows
    line = lax.broadcasted_iota(jnp.int32, (rows, rows), 0) + mine
    sign = jnp.where(line == mate_ref[...], jnp.float32(1.0), jnp.float32(-1.0))
    coef = -sign * jax.nn.sigmoid(-sign * (scale * logits + offset)) * share
    for kind, tile in ((1, coef), (0, coef.T)):
        high, low = split(tile)
        total = dot(high, high_ref[1 - kind])
        total += dot(high, low_ref[1 - kind])
        total += dot(low, high_ref[1 - kind])
        out_ref[kind] = total

    def multiply(slot, kind, index):
        block = buf[slot, pl.ds(pl.multiple_of(index * part, part), part), :]
        high, low = split(block)
        both = jnp.concatenate([high, low], axis=0)
        twice = dot_nt(high_ref[kind], both)
        logits = twice[:, :part] + twice[:, part:] + dot_nt(low_ref[kind], high)
        coef = jax.nn.sigmoid(scale * logits + offset) * share
        coef_high, coef_low = split(coef)
        out_ref[kind] += dot(
            jnp.concatenate([coef_high, coef_low, coef_high], axis=1),
            jnp.concatenate([high, high, low], axis=0),
        )

    def step(i, carry):
        issue(i + AHEAD)

        @pl.when(is_outer & (i < PIECES))
        def _():
            arrived(PASS_P, i)
            flows[2](i).start()
            flows[3](i).start()

        late = i - LAG

        @pl.when((late >= 0) & (late < PIECES))
        def _():
            arrived(A2, late)
            flows[7](late).start()
            arrived(A4, late)

            @pl.when(core != side)
            def _():
                flows[9](late).start()

        @pl.when((late >= PIECES) & (late < 2 * PIECES))
        def _():
            index = late - PIECES
            arrived(B2, index)
            flows[8](index).start()
            arrived(B4, index)

            @pl.when(core == side)
            def _():
                flows[9](index).start()

        item = late - PER

        @pl.when(item >= 0)
        def _():
            half = item // PIECES
            index = item // PER - half * PARTS
            turn = item % PER
            spare = jnp.where((core == side) == (half == 0), X4S, SIB)
            slot = jnp.where(
                half == 0,
                jnp.where(turn == 0, A2, jnp.where(turn == 1, A4, jnp.where(turn == 2, A2S, spare))),
                jnp.where(turn == 0, B2, jnp.where(turn == 1, B4, jnp.where(turn == 2, B2S, spare))),
            )
            type_2 = jnp.where(half == 0, type_a2, type_b2)
            type_4 = jnp.where(half == 0, near, far)
            kind = jnp.where(
                turn % 2 == 0, type_2, jnp.where((turn == 3) & (spare == SIB), 1 - core, type_4)
            )

            @pl.when(turn >= 2)
            def _():
                for k in range(PER):
                    arrived(slot, index * PER + k)

            multiply(slot, kind, index)

        return carry

    lax.fori_loop(0, 2 * PIECES + LAG + PER, step, 0)

    def finish(i, carry):
        for flow in (0, 1, 4, 5, 6, 7, 8, 9):
            flows[flow](i).wait_send()

        @pl.when(is_outer)
        def _():
            flows[2](i).wait_send()
            flows[3](i).wait_send()

        return carry

    lax.fori_loop(0, PIECES, finish, 0)


def body(photo_embedding_matrix, caption_embedding_matrix, caption_mate_entry, sharpness_factor, affinity_offset):
    rows, width = photo_embedding_matrix.shape
    planes = lax.axis_size("dp") // 2
    both = pl.pallas_call(
        functools.partial(kernel, planes),
        out_shape=jax.ShapeDtypeStruct((2, rows, width), jnp.float32),
        in_specs=[
            pl.BlockSpec(memory_space=pl.ANY),
            pl.BlockSpec(memory_space=pl.ANY),
            pl.BlockSpec(memory_space=pltpu.VMEM),
            pl.BlockSpec(memory_space=pltpu.SMEM),
            pl.BlockSpec(memory_space=pltpu.SMEM),
        ],
        out_specs=pl.BlockSpec(memory_space=pltpu.VMEM),
        scratch_shapes=[
            pltpu.VMEM((SLOTS, rows, width), jnp.float32),
            pltpu.VMEM((2, rows, width), jnp.bfloat16),
            pltpu.VMEM((2, rows, width), jnp.bfloat16),
            pltpu.SemaphoreType.DMA((10, PIECES)),
            pltpu.SemaphoreType.DMA((SLOTS, PIECES)),
            pltpu.SemaphoreType.DMA((2,)),
        ],
        compiler_params=pltpu.CompilerParams(
            collective_id=0, has_side_effects=True, vmem_limit_bytes=56 * 1024 * 1024
        ),
        cost_estimate=pl.CostEstimate(
            flops=57 * 2 * rows * rows * width,
            bytes_accessed=16 * rows * width,
            transcendentals=9 * rows * rows,
        ),
    )(
        caption_embedding_matrix,
        photo_embedding_matrix,
        caption_mate_entry.reshape(1, rows),
        sharpness_factor,
        affinity_offset,
    )
    return both[0], both[1]


def solution(mesh):
    in_specs = (P(("dp", "mp"), None), P(("dp", "mp"), None), P(("dp", "mp")), P(), P())
    out_specs = (P(("dp", "mp"), None), P(("dp", "mp"), None))
    return jax.shard_map(body, mesh=mesh, in_specs=in_specs, out_specs=out_specs, check_vma=False)
```

```python
import functools

import jax
import jax.numpy as jnp
from jax import lax
from jax.experimental import pallas as pl
from jax.experimental.pallas import tpu as pltpu
from jax.sharding import PartitionSpec as P

HOPS = 4
PIECES = 12
AHEAD = 2
LAG = 2
TEXT, IMAGE, SIB, A2, A4, B2, B4, A2S, B2S, X4S, PASS_P, PASS_Q = range(12)
SLOTS = 12
NT = (((1,), (1,)), ((), ()))


def split(value):
    high = value.astype(jnp.bfloat16)
    return high, (value - high.astype(jnp.float32)).astype(jnp.bfloat16)


def dot(left, right):
    return jnp.dot(left, right, preferred_element_type=jnp.float32)


def dot_nt(left, right):
    return lax.dot_general(left, right, NT, preferred_element_type=jnp.float32)


def kernel(
    planes, text_ref, image_ref, mate_ref, scale_ref, offset_ref, out_ref,
    buf, high_ref, low_ref, mate_buf, send_sem, recv_sem, load_sem,
):
    rows = text_ref.shape[0]
    piece = rows // PIECES
    dp, mp = lax.axis_index("dp"), lax.axis_index("mp")
    plane, x_lo = dp // 2, dp % 2
    side, core = mp // 2, mp % 2
    outer = jnp.where(x_lo == side, 1, 0)
    is_outer = x_lo == side
    near, far = side, 1 - side
    type_a2 = jnp.where(is_outer, far, near)
    type_b2 = jnp.where(is_outer, near, far)

    def at(z, lo, hi, c):
        return (z * 2 + lo, hi * 2 + c)

    beside = at(plane, 1 - x_lo, side, core)
    across = at(plane, 1 - x_lo, 1 - side, core)
    sibling = at(plane, x_lo, side, 1 - core)
    up = at((plane + 1) % planes, x_lo, side, core)
    down = at((plane + planes - 1) % planes, x_lo, side, core)

    def pick(flag, yes, no):
        return tuple(jnp.where(flag, a, b) for a, b in zip(yes, no))

    z_near = pick(side == 0, up, down)
    z_far = pick(side == 0, down, up)

    def move(flow, source, target, index, device):
        lines = pl.ds(pl.multiple_of(index * piece, piece), piece)
        return pltpu.make_async_remote_copy(
            src_ref=buf.at[source, lines],
            dst_ref=buf.at[target, lines],
            send_sem=send_sem.at[flow, index],
            recv_sem=recv_sem.at[target, index],
            device_id=device,
            device_id_type=pl.DeviceIdType.MESH,
        )

    def arrived(slot, index):
        move(0, slot, slot, index, sibling).wait_recv()

    first_target = jnp.where(is_outer, A4, PASS_P)
    second_target = jnp.where(is_outer, PASS_Q, A2)
    second_device = pick(is_outer, z_far, across)
    third_source = jnp.where(is_outer, PASS_Q, A4)
    fourth_source = jnp.where(is_outer, PASS_Q, far)

    flows = [
        lambda i: move(0, near, first_target, i, beside),
        lambda i: move(1, far, second_target, i, second_device),
        lambda i: move(2, PASS_P, A2, i, across),
        lambda i: move(3, PASS_P, A4, i, z_near),
        lambda i: move(4, third_source, B2, i, across),
        lambda i: move(5, fourth_source, B4, i, beside),
        lambda i: move(6, core, SIB, i, sibling),
        lambda i: move(7, A2, A2S, i, sibling),
        lambda i: move(8, B2, B2S, i, sibling),
        lambda i: move(9, jnp.where(core == side, B4, A4), X4S, i, sibling),
    ]

    load_text = pltpu.make_async_copy(text_ref, buf.at[TEXT], load_sem.at[0])
    load_image = pltpu.make_async_copy(image_ref, buf.at[IMAGE], load_sem.at[1])
    load_mate = pltpu.make_async_copy(mate_ref, mate_buf, load_sem.at[2])
    load_text.start()
    load_image.start()
    load_mate.start()

    barrier = pltpu.get_barrier_semaphore()

    def greet(device):
        pl.semaphore_signal(barrier, inc=1, device_id=device, device_id_type=pl.DeviceIdType.MESH)

    for device in (beside, across, sibling):
        greet(device)

    @pl.when(is_outer)
    def _():
        greet(up)
        greet(down)

    out_ref[...] = jnp.zeros_like(out_ref)
    load_text.wait()
    load_image.wait()
    load_mate.wait()
    pl.semaphore_wait(barrier, 3 + 2 * outer)

    def issue(step):
        @pl.when(step < PIECES)
        def _():
            flows[0](step).start()
            flows[1](step).start()
            flows[6](step).start()

        @pl.when((step >= PIECES) & (step < 2 * PIECES))
        def _():
            index = step - PIECES

            @pl.when(is_outer)
            def _():
                arrived(PASS_Q, index)

            flows[4](index).start()
            flows[5](index).start()

    lax.fori_loop(0, AHEAD, lambda i, c: (issue(i), c)[1], 0)

    scale = scale_ref[0]
    offset = offset_ref[0]
    share = scale * jnp.float32(1.0 / (HOPS + 1))

    for kind, slot in ((0, IMAGE), (1, TEXT)):
        high, low = split(buf[slot])
        high_ref[kind] = high
        low_ref[kind] = low

    def diagonal():
        logits = dot_nt(high_ref[1], high_ref[0])
        logits += dot_nt(high_ref[1], low_ref[0])
        logits += dot_nt(low_ref[1], high_ref[0])
        mine = (dp * 4 + mp) * rows
        line = lax.broadcasted_iota(jnp.int32, (rows, rows), 0) + mine
        sign = jnp.where(line == mate_buf[...].reshape(1, rows), jnp.float32(1.0), jnp.float32(-1.0))
        coef = -sign * jax.nn.sigmoid(-sign * (scale * logits + offset)) * share
        for kind, tile in ((1, coef), (0, coef.T)):
            high, low = split(tile)
            total = dot(high, high_ref[1 - kind])
            total += dot(high, low_ref[1 - kind])
            total += dot(low, high_ref[1 - kind])
            out_ref[kind] += total

    def multiply(one, other, kind, index):
        lines = pl.ds(pl.multiple_of(index * 2 * piece, 2 * piece), 2 * piece)
        block = jnp.concatenate([buf[one, lines], buf[other, lines]], axis=0)
        high, low = split(block)
        both = jnp.concatenate([high, low], axis=0)
        twice = dot_nt(high_ref[kind], both)
        logits = twice[:, : 4 * piece] + twice[:, 4 * piece :] + dot_nt(low_ref[kind], high)
        coef = jax.nn.sigmoid(scale * logits + offset) * share
        coef_high, coef_low = split(coef)
        out_ref[kind] += dot(
            jnp.concatenate([coef_high, coef_low, coef_high], axis=1),
            jnp.concatenate([high, high, low], axis=0),
        )

    def step(i, carry):
        issue(i + AHEAD)

        @pl.when(is_outer & (i < PIECES))
        def _():
            arrived(PASS_P, i)
            flows[2](i).start()
            flows[3](i).start()

        item = i - 2 - LAG

        @pl.when(item >= 0)
        def _():
            half = item // PIECES
            index = (item - half * PIECES) // 2
            spare = jnp.where((core == side) == (half == 0), X4S, SIB)
            first = item % 2 == 0
            one = jnp.where(half == 0, jnp.where(first, A2, A4), jnp.where(first, B2, B4))
            other = jnp.where(first, jnp.where(half == 0, A2S, B2S), spare)
            kind = jnp.where(
                first, jnp.where(half == 0, type_a2, type_b2), jnp.where(half == 0, near, far)
            )
            arrived(other, 2 * index)
            arrived(other, 2 * index + 1)
            multiply(one, other, kind, index)

        late = i - LAG

        @pl.when((late >= 0) & (late < PIECES))
        def _():
            arrived(A2, late)
            flows[7](late).start()
            arrived(A4, late)

            @pl.when(core != side)
            def _():
                flows[9](late).start()

        @pl.when((late >= PIECES) & (late < 2 * PIECES))
        def _():
            index = late - PIECES
            arrived(B2, index)
            flows[8](index).start()
            arrived(B4, index)

            @pl.when(core == side)
            def _():
                flows[9](index).start()

        @pl.when(i == PIECES + 1)
        def _():
            diagonal()

        return carry

    lax.fori_loop(0, 2 * PIECES + LAG + 2, step, 0)

    def finish(i, carry):
        for flow in (0, 1, 4, 5, 6, 7, 8, 9):
            flows[flow](i).wait_send()

        @pl.when(is_outer)
        def _():
            flows[2](i).wait_send()
            flows[3](i).wait_send()

        return carry

    lax.fori_loop(0, PIECES, finish, 0)


def body(photo_embedding_matrix, caption_embedding_matrix, caption_mate_entry, sharpness_factor, affinity_offset):
    rows, width = photo_embedding_matrix.shape
    planes = lax.axis_size("dp") // 2
    both = pl.pallas_call(
        functools.partial(kernel, planes),
        out_shape=pltpu.VMEM((2, rows, width), jnp.float32),
        in_specs=[
            pl.BlockSpec(memory_space=pltpu.HBM),
            pl.BlockSpec(memory_space=pltpu.HBM),
            pl.BlockSpec(memory_space=pltpu.HBM),
            pl.BlockSpec(memory_space=pltpu.SMEM),
            pl.BlockSpec(memory_space=pltpu.SMEM),
        ],
        out_specs=pl.BlockSpec(memory_space=pltpu.VMEM),
        scratch_shapes=[
            pltpu.VMEM((SLOTS, rows, width), jnp.float32),
            pltpu.VMEM((2, rows, width), jnp.bfloat16),
            pltpu.VMEM((2, rows, width), jnp.bfloat16),
            pltpu.VMEM((rows,), jnp.int32),
            pltpu.SemaphoreType.DMA((10, PIECES)),
            pltpu.SemaphoreType.DMA((SLOTS, PIECES)),
            pltpu.SemaphoreType.DMA((3,)),
        ],
        compiler_params=pltpu.CompilerParams(
            collective_id=0, has_side_effects=True, vmem_limit_bytes=48 * 1024 * 1024
        ),
        cost_estimate=pl.CostEstimate(
            flops=57 * 2 * rows * rows * width,
            bytes_accessed=16 * rows * width,
            transcendentals=9 * rows * rows,
        ),
    )(
        pltpu.with_memory_space_constraint(caption_embedding_matrix, pltpu.HBM),
        pltpu.with_memory_space_constraint(photo_embedding_matrix, pltpu.HBM),
        pltpu.with_memory_space_constraint(caption_mate_entry, pltpu.HBM),
        sharpness_factor,
        affinity_offset,
    )
    return both[0], both[1]


def solution(mesh):
    in_specs = (P(("dp", "mp"), None), P(("dp", "mp"), None), P(("dp", "mp")), P(), P())
    out_specs = (P(("dp", "mp"), None), P(("dp", "mp"), None))
    return jax.shard_map(body, mesh=mesh, in_specs=in_specs, out_specs=out_specs, check_vma=False)
```

```python
import functools

import jax
import jax.numpy as jnp
from jax import lax
from jax.experimental import pallas as pl
from jax.experimental.pallas import tpu as pltpu
from jax.sharding import PartitionSpec as P

HOPS = 4
PIECES = 12
AHEAD = 2
LAG_INNER = 2
LAG_OUTER = 4
TRAIL = 1
SLIVERS = 2
EARLY = 1
EARLY_AT = 6
TEXT, IMAGE, SIB, A2, A4, B2, B4, A2S, B2S, X4S, PASS_P, PASS_Q = range(12)
SLOTS = 12
NT = (((1,), (1,)), ((), ()))


def split(value):
    high = value.astype(jnp.bfloat16)
    return high, (value - high.astype(jnp.float32)).astype(jnp.bfloat16)


def dot(left, right):
    return jnp.dot(left, right, preferred_element_type=jnp.float32)


def dot_nt(left, right):
    return lax.dot_general(left, right, NT, preferred_element_type=jnp.float32)


def kernel(
    planes, text_ref, image_ref, mate_ref, scale_ref, offset_ref, out_ref,
    buf, high_ref, low_ref, mate_buf, send_sem, recv_sem, load_sem, sliver_sem, go_sem,
):
    rows = text_ref.shape[0]
    piece = rows // PIECES
    dp, mp = lax.axis_index("dp"), lax.axis_index("mp")
    plane, x_lo = dp // 2, dp % 2
    side, core = mp // 2, mp % 2
    is_outer = x_lo == side
    lag = jnp.where(is_outer, LAG_OUTER, LAG_INNER)
    near, far = side, 1 - side
    type_a2 = jnp.where(is_outer, far, near)
    type_b2 = jnp.where(is_outer, near, far)

    def at(z, lo, hi, c):
        return (z * 2 + lo, hi * 2 + c)

    beside = at(plane, 1 - x_lo, side, core)
    across = at(plane, 1 - x_lo, 1 - side, core)
    sibling = at(plane, x_lo, side, 1 - core)
    up = at((plane + 1) % planes, x_lo, side, core)
    down = at((plane + planes - 1) % planes, x_lo, side, core)

    def pick(flag, yes, no):
        return tuple(jnp.where(flag, a, b) for a, b in zip(yes, no))

    z_near = pick(side == 0, up, down)
    z_far = pick(side == 0, down, up)

    def move(flow, source, target, index, device):
        lines = pl.ds(pl.multiple_of(index * piece, piece), piece)
        return pltpu.make_async_remote_copy(
            src_ref=buf.at[source, lines],
            dst_ref=buf.at[target, lines],
            send_sem=send_sem.at[flow, index],
            recv_sem=recv_sem.at[target, index],
            device_id=device,
            device_id_type=pl.DeviceIdType.MESH,
        )

    def arrived(slot, index):
        move(0, slot, slot, index, sibling).wait_recv()

    first_target = jnp.where(is_outer, A4, PASS_P)
    second_target = jnp.where(is_outer, PASS_Q, A2)
    second_device = pick(is_outer, z_far, across)
    third_source = jnp.where(is_outer, PASS_Q, A4)
    fourth_source = jnp.where(is_outer, PASS_Q, far)

    flows = [
        lambda i: move(0, near, first_target, i, beside),
        lambda i: move(1, far, second_target, i, second_device),
        lambda i: move(2, PASS_P, A2, i, across),
        lambda i: move(3, PASS_P, A4, i, z_near),
        lambda i: move(4, third_source, B2, i, across),
        lambda i: move(5, fourth_source, B4, i, beside),
        lambda i: move(6, core, SIB, i, sibling),
        lambda i: move(7, A2, A2S, i, sibling),
        lambda i: move(8, B2, B2S, i, sibling),
        lambda i: move(9, jnp.where(core == side, B4, A4), X4S, i, sibling),
    ]

    load_text = pltpu.make_async_copy(text_ref, buf.at[TEXT], load_sem.at[0])
    load_image = pltpu.make_async_copy(image_ref, buf.at[IMAGE], load_sem.at[1])
    load_mate = pltpu.make_async_copy(mate_ref, mate_buf, load_sem.at[2])
    load_text.start()
    load_image.start()
    load_mate.start()

    barrier = pltpu.get_barrier_semaphore()

    def signal(semaphore, device):
        pl.semaphore_signal(semaphore, inc=1, device_id=device, device_id_type=pl.DeviceIdType.MESH)

    @pl.when(is_outer)
    def _():
        signal(barrier, beside)
        signal(barrier, at(plane, 1 - x_lo, side, 1 - core))
        signal(barrier, at(plane, x_lo, 1 - side, core))
        signal(barrier, up)
        signal(barrier, down)

    @pl.when(x_lo != side)
    def _():
        signal(barrier, across)
        signal(barrier, sibling)
        pl.semaphore_wait(barrier, 5)
        signal(go_sem, beside)

    @pl.when(is_outer)
    def _():
        pl.semaphore_wait(go_sem, 1)

    def begin(ref, flow, target, index, device):
        lines = pl.ds(index * piece, piece)
        pltpu.make_async_remote_copy(
            src_ref=ref.at[lines],
            dst_ref=buf.at[target, lines],
            send_sem=send_sem.at[flow, index],
            recv_sem=recv_sem.at[target, index],
            device_id=device,
            device_id_type=pl.DeviceIdType.MESH,
        ).start()

    thin = piece // SLIVERS

    def sliver(ref, flow, target, index, part, recv, device):
        lines = pl.ds(pl.multiple_of(index * piece + part * thin, thin), thin)
        return pltpu.make_async_remote_copy(
            src_ref=ref.at[lines],
            dst_ref=buf.at[target, lines],
            send_sem=send_sem.at[flow, index],
            recv_sem=recv,
            device_id=device,
            device_id_type=pl.DeviceIdType.MESH,
        )

    def begin_slivers(ref, index):
        for part in range(SLIVERS):
            sliver(ref, 0, PASS_P, index, part, sliver_sem.at[index * SLIVERS + part], beside).start()

    def relay(index):
        for part in range(SLIVERS):
            source = buf.at[PASS_P]
            sliver(source, 2, PASS_P, index, part, sliver_sem.at[index * SLIVERS + part], across).wait_recv()
            sliver(source, 2, A2, index, part, recv_sem.at[A2, index], across).start()

    for which, near_ref, far_ref in ((0, text_ref, image_ref), (1, image_ref, text_ref)):

        @pl.when((side == which) & is_outer)
        def _(near_ref=near_ref):
            for index in range(AHEAD):
                begin(near_ref, 0, A4, index, beside)

        @pl.when((side == which) & (x_lo != side))
        def _(near_ref=near_ref, far_ref=far_ref):
            for index in range(AHEAD):
                begin_slivers(near_ref, index)
                begin(far_ref, 1, A2, index, across)

    out_ref[...] = jnp.zeros_like(out_ref)

    @pl.when(is_outer)
    def _():
        relay(0)

    load_text.wait()
    load_image.wait()
    load_mate.wait()

    def issue(step):
        @pl.when((step < PIECES) & is_outer)
        def _():
            flows[0](step).start()

        @pl.when((step < PIECES) & (x_lo != side))
        def _():
            begin_slivers(buf.at[near], step)
            flows[1](step).start()

        @pl.when((step >= PIECES) & (step < 2 * PIECES))
        def _():
            index = step - PIECES

            @pl.when(is_outer & (index >= EARLY))
            def _():
                arrived(PASS_Q, index)

            @pl.when((x_lo != side) | (index >= EARLY))
            def _():
                flows[4](index).start()

            flows[5](index).start()

    scale = scale_ref[0]
    offset = offset_ref[0]
    share = scale * jnp.float32(1.0 / (HOPS + 1))

    for kind, slot in ((0, IMAGE), (1, TEXT)):
        high, low = split(buf[slot])
        high_ref[kind] = high
        low_ref[kind] = low

    def diagonal():
        logits = dot_nt(high_ref[1], high_ref[0])
        logits += dot_nt(high_ref[1], low_ref[0])
        logits += dot_nt(low_ref[1], high_ref[0])
        mine = (dp * 4 + mp) * rows
        line = lax.broadcasted_iota(jnp.int32, (rows, rows), 0) + mine
        sign = jnp.where(line == mate_buf[...].reshape(1, rows), jnp.float32(1.0), jnp.float32(-1.0))
        coef = -sign * jax.nn.sigmoid(-sign * (scale * logits + offset)) * share
        for kind, tile in ((1, coef), (0, coef.T)):
            high, low = split(tile)
            total = dot(high, high_ref[1 - kind])
            total += dot(high, low_ref[1 - kind])
            total += dot(low, high_ref[1 - kind])
            out_ref[kind] += total

    def multiply(one, other, kind, index):
        lines = pl.ds(pl.multiple_of(index * 2 * piece, 2 * piece), 2 * piece)
        block = jnp.concatenate([buf[one, lines], buf[other, lines]], axis=0)
        high, low = split(block)
        both = jnp.concatenate([high, low], axis=0)
        twice = dot_nt(high_ref[kind], both)
        logits = twice[:, : 4 * piece] + twice[:, 4 * piece :] + dot_nt(low_ref[kind], high)
        coef = jax.nn.sigmoid(scale * logits + offset) * share
        coef_high, coef_low = split(coef)
        out_ref[kind] += dot(
            jnp.concatenate([coef_high, coef_low, coef_high], axis=1),
            jnp.concatenate([high, high, low], axis=0),
        )

    def step(i, carry):
        issue(i + AHEAD)

        @pl.when(i < PIECES)
        def _():
            flows[6](i).start()

        @pl.when(is_outer & (i >= 1) & (i < PIECES))
        def _():
            relay(i)

        @pl.when(is_outer & (i == TRAIL))
        def _():
            pl.semaphore_wait(barrier, 2)

        @pl.when(is_outer & (i >= TRAIL) & (i < PIECES + TRAIL))
        def _():
            flows[1](i - TRAIL).start()
            flows[3](i - TRAIL).start()

        @pl.when(is_outer & (i >= EARLY_AT) & (i < EARLY_AT + EARLY))
        def _():
            arrived(PASS_Q, i - EARLY_AT)
            flows[4](i - EARLY_AT).start()

        item = i - 2 - lag

        @pl.when((item >= 0) & (item < 2 * PIECES))
        def _():
            half = item // PIECES
            index = (item - half * PIECES) // 2
            spare = jnp.where((core == side) == (half == 0), X4S, SIB)
            first = item % 2 == 0
            one = jnp.where(half == 0, jnp.where(first, A2, A4), jnp.where(first, B2, B4))
            other = jnp.where(first, jnp.where(half == 0, A2S, B2S), spare)
            kind = jnp.where(
                first, jnp.where(half == 0, type_a2, type_b2), jnp.where(half == 0, near, far)
            )
            arrived(other, 2 * index)
            arrived(other, 2 * index + 1)
            multiply(one, other, kind, index)

        late = i - lag

        @pl.when((late >= 0) & (late < PIECES))
        def _():
            arrived(A2, late)
            flows[7](late).start()
            arrived(A4, late)

            @pl.when(core != side)
            def _():
                flows[9](late).start()

        @pl.when((late >= PIECES) & (late < 2 * PIECES))
        def _():
            index = late - PIECES
            arrived(B2, index)
            flows[8](index).start()
            arrived(B4, index)

            @pl.when(core == side)
            def _():
                flows[9](index).start()

        @pl.when(i == PIECES + 1)
        def _():
            diagonal()

        return carry

    lax.fori_loop(0, 2 * PIECES + LAG_OUTER + 2, step, 0)

    def finish(i, carry):
        for flow in (0, 1, 4, 5, 6, 7, 8, 9):
            flows[flow](i).wait_send()

        @pl.when(is_outer)
        def _():
            flows[2](i).wait_send()
            flows[3](i).wait_send()

        return carry

    lax.fori_loop(0, PIECES, finish, 0)


def body(photo_embedding_matrix, caption_embedding_matrix, caption_mate_entry, sharpness_factor, affinity_offset):
    rows, width = photo_embedding_matrix.shape
    planes = lax.axis_size("dp") // 2
    both = pl.pallas_call(
        functools.partial(kernel, planes),
        out_shape=pltpu.VMEM((2, rows, width), jnp.float32),
        in_specs=[
            pl.BlockSpec(memory_space=pltpu.HBM),
            pl.BlockSpec(memory_space=pltpu.HBM),
            pl.BlockSpec(memory_space=pltpu.HBM),
            pl.BlockSpec(memory_space=pltpu.SMEM),
            pl.BlockSpec(memory_space=pltpu.SMEM),
        ],
        out_specs=pl.BlockSpec(memory_space=pltpu.VMEM),
        scratch_shapes=[
            pltpu.VMEM((SLOTS, rows, width), jnp.float32),
            pltpu.VMEM((2, rows, width), jnp.bfloat16),
            pltpu.VMEM((2, rows, width), jnp.bfloat16),
            pltpu.VMEM((rows,), jnp.int32),
            pltpu.SemaphoreType.DMA((10, PIECES)),
            pltpu.SemaphoreType.DMA((SLOTS, PIECES)),
            pltpu.SemaphoreType.DMA((3,)),
            pltpu.SemaphoreType.DMA((PIECES * SLIVERS,)),
            pltpu.SemaphoreType.REGULAR,
        ],
        compiler_params=pltpu.CompilerParams(
            collective_id=0, has_side_effects=True, vmem_limit_bytes=48 * 1024 * 1024
        ),
        cost_estimate=pl.CostEstimate(
            flops=57 * 2 * rows * rows * width,
            bytes_accessed=16 * rows * width,
            transcendentals=9 * rows * rows,
        ),
    )(
        pltpu.with_memory_space_constraint(caption_embedding_matrix, pltpu.HBM),
        pltpu.with_memory_space_constraint(photo_embedding_matrix, pltpu.HBM),
        pltpu.with_memory_space_constraint(caption_mate_entry, pltpu.HBM),
        sharpness_factor,
        affinity_offset,
    )
    return both[0], both[1]


def solution(mesh):
    in_specs = (P(("dp", "mp"), None), P(("dp", "mp"), None), P(("dp", "mp")), P(), P())
    out_specs = (P(("dp", "mp"), None), P(("dp", "mp"), None))
    return jax.shard_map(body, mesh=mesh, in_specs=in_specs, out_specs=out_specs, check_vma=False)
```

```python
import functools

import jax
import jax.numpy as jnp
from jax import lax
from jax.experimental import pallas as pl
from jax.experimental.pallas import tpu as pltpu
from jax.sharding import PartitionSpec as P

HOPS = 4
PIECES = 12
AHEAD = 2
LAG_INNER = 2
LAG_OUTER = 4
TRAIL = 0
SLIVERS = 2
EARLY = 1
EARLY_AT = 6
DETOUR = 3
DETOUR_AT = 7
TEXT, IMAGE, SIB, A2, A4, B2, B4, A2S, B2S, X4S, PASS_P, PASS_Q = range(12)
SLOTS = 12
NT = (((1,), (1,)), ((), ()))


def split(value):
    high = value.astype(jnp.bfloat16)
    return high, (value - high.astype(jnp.float32)).astype(jnp.bfloat16)


def dot(left, right):
    return jnp.dot(left, right, preferred_element_type=jnp.float32)


def dot_nt(left, right):
    return lax.dot_general(left, right, NT, preferred_element_type=jnp.float32)


def kernel(
    planes, text_ref, image_ref, mate_ref, scale_ref, offset_ref, out_ref,
    buf, high_ref, low_ref, mate_buf, send_sem, recv_sem, load_sem, sliver_sem, go_sem,
):
    rows = text_ref.shape[0]
    piece = rows // PIECES
    dp, mp = lax.axis_index("dp"), lax.axis_index("mp")
    plane, x_lo = dp // 2, dp % 2
    side, core = mp // 2, mp % 2
    is_outer = x_lo == side
    lag = jnp.where(is_outer, LAG_OUTER, LAG_INNER)
    near, far = side, 1 - side
    type_a2 = jnp.where(is_outer, far, near)
    type_b2 = jnp.where(is_outer, near, far)

    def at(z, lo, hi, c):
        return (z * 2 + lo, hi * 2 + c)

    beside = at(plane, 1 - x_lo, side, core)
    across = at(plane, 1 - x_lo, 1 - side, core)
    sibling = at(plane, x_lo, side, 1 - core)
    up = at((plane + 1) % planes, x_lo, side, core)
    down = at((plane + planes - 1) % planes, x_lo, side, core)

    def pick(flag, yes, no):
        return tuple(jnp.where(flag, a, b) for a, b in zip(yes, no))

    z_near = pick(side == 0, up, down)
    z_far = pick(side == 0, down, up)

    def move(flow, source, target, index, device):
        lines = pl.ds(pl.multiple_of(index * piece, piece), piece)
        return pltpu.make_async_remote_copy(
            src_ref=buf.at[source, lines],
            dst_ref=buf.at[target, lines],
            send_sem=send_sem.at[flow, index],
            recv_sem=recv_sem.at[target, index],
            device_id=device,
            device_id_type=pl.DeviceIdType.MESH,
        )

    def arrived(slot, index):
        move(0, slot, slot, index, sibling).wait_recv()

    first_target = jnp.where(is_outer, A4, PASS_P)
    second_target = jnp.where(is_outer, PASS_Q, A2)
    second_device = pick(is_outer, z_far, across)
    third_source = jnp.where(is_outer, PASS_Q, A4)
    fourth_source = jnp.where(is_outer, PASS_Q, far)

    flows = [
        lambda i: move(0, near, first_target, i, beside),
        lambda i: move(1, far, second_target, i, second_device),
        lambda i: move(2, PASS_P, A2, i, across),
        lambda i: move(3, PASS_P, A4, i, z_near),
        lambda i: move(4, third_source, B2, i, across),
        lambda i: move(5, fourth_source, B4, i, beside),
        lambda i: move(6, core, SIB, i, sibling),
        lambda i: move(7, A2, A2S, i, sibling),
        lambda i: move(8, B2, B2S, i, sibling),
        lambda i: move(9, jnp.where(core == side, B4, A4), X4S, i, sibling),
    ]

    load_text = pltpu.make_async_copy(text_ref, buf.at[TEXT], load_sem.at[0])
    load_image = pltpu.make_async_copy(image_ref, buf.at[IMAGE], load_sem.at[1])
    load_mate = pltpu.make_async_copy(mate_ref, mate_buf, load_sem.at[2])
    load_text.start()
    load_image.start()
    load_mate.start()

    barrier = pltpu.get_barrier_semaphore()

    def signal(semaphore, device):
        pl.semaphore_signal(semaphore, inc=1, device_id=device, device_id_type=pl.DeviceIdType.MESH)

    @pl.when(is_outer)
    def _():
        signal(barrier, beside)
        signal(barrier, at(plane, 1 - x_lo, side, 1 - core))
        signal(barrier, at(plane, x_lo, 1 - side, core))
        signal(barrier, up)
        signal(barrier, down)

    @pl.when(x_lo != side)
    def _():
        signal(barrier, across)
        signal(barrier, sibling)
        pl.semaphore_wait(barrier, 5)
        signal(go_sem, beside)

    @pl.when(is_outer)
    def _():
        pl.semaphore_wait(go_sem, 1)

    def begin(ref, flow, target, index, device):
        lines = pl.ds(index * piece, piece)
        pltpu.make_async_remote_copy(
            src_ref=ref.at[lines],
            dst_ref=buf.at[target, lines],
            send_sem=send_sem.at[flow, index],
            recv_sem=recv_sem.at[target, index],
            device_id=device,
            device_id_type=pl.DeviceIdType.MESH,
        ).start()

    thin = piece // SLIVERS

    def sliver(ref, flow, target, index, part, recv, device):
        lines = pl.ds(pl.multiple_of(index * piece + part * thin, thin), thin)
        return pltpu.make_async_remote_copy(
            src_ref=ref.at[lines],
            dst_ref=buf.at[target, lines],
            send_sem=send_sem.at[flow, index],
            recv_sem=recv,
            device_id=device,
            device_id_type=pl.DeviceIdType.MESH,
        )

    def begin_slivers(ref, index):
        for part in range(SLIVERS):
            sliver(ref, 0, PASS_P, index, part, sliver_sem.at[index * SLIVERS + part], beside).start()

    last = PIECES - 1
    kept = piece - piece * DETOUR // 4

    def detour(source, flow, target, recv, device):
        lines = pl.ds(last * piece + kept, piece - kept)
        return pltpu.make_async_remote_copy(
            src_ref=buf.at[source, lines],
            dst_ref=buf.at[target, lines],
            send_sem=send_sem.at[flow, last],
            recv_sem=recv,
            device_id=device,
            device_id_type=pl.DeviceIdType.MESH,
        )

    out_way = detour(near, 2, PASS_P, recv_sem.at[PASS_P, last], across)
    in_way = detour(PASS_P, 3, A2, recv_sem.at[A2, last], beside)
    lines_kept = pl.ds(last * piece, kept)
    straight = pltpu.make_async_remote_copy(
        src_ref=buf.at[PASS_P, lines_kept],
        dst_ref=buf.at[A2, lines_kept],
        send_sem=send_sem.at[2, last],
        recv_sem=recv_sem.at[A2, last],
        device_id=across,
        device_id_type=pl.DeviceIdType.MESH,
    )

    def relay_last():
        for part in range(SLIVERS):
            recv = sliver_sem.at[last * SLIVERS + part]
            sliver(buf.at[PASS_P], 2, PASS_P, last, part, recv, across).wait_recv()
        straight.start()

    def relay(index):
        for part in range(SLIVERS):
            source = buf.at[PASS_P]
            sliver(source, 2, PASS_P, index, part, sliver_sem.at[index * SLIVERS + part], across).wait_recv()
            sliver(source, 2, A2, index, part, recv_sem.at[A2, index], across).start()

    for which, near_ref, far_ref in ((0, text_ref, image_ref), (1, image_ref, text_ref)):

        @pl.when((side == which) & is_outer)
        def _(near_ref=near_ref):
            for index in range(AHEAD):
                begin(near_ref, 0, A4, index, beside)

        @pl.when((side == which) & (x_lo != side))
        def _(near_ref=near_ref, far_ref=far_ref):
            for index in range(AHEAD):
                begin_slivers(near_ref, index)
                begin(far_ref, 1, A2, index, across)

    out_ref[...] = jnp.zeros_like(out_ref)

    @pl.when(is_outer)
    def _():
        relay(0)

    load_text.wait()
    load_image.wait()
    load_mate.wait()

    def issue(step):
        @pl.when((step < PIECES) & is_outer)
        def _():
            flows[0](step).start()

        @pl.when((step < PIECES) & (x_lo != side))
        def _():
            begin_slivers(buf.at[near], step)
            flows[1](step).start()

        @pl.when((step >= PIECES) & (step < 2 * PIECES))
        def _():
            index = step - PIECES

            @pl.when(is_outer & (index >= EARLY))
            def _():
                arrived(PASS_Q, index)

            @pl.when((x_lo != side) | (index >= EARLY))
            def _():
                flows[4](index).start()

            flows[5](index).start()

    scale = scale_ref[0]
    offset = offset_ref[0]
    share = scale * jnp.float32(1.0 / (HOPS + 1))

    for kind, slot in ((0, IMAGE), (1, TEXT)):
        high, low = split(buf[slot])
        high_ref[kind] = high
        low_ref[kind] = low

    def diagonal():
        logits = dot_nt(high_ref[1], high_ref[0])
        logits += dot_nt(high_ref[1], low_ref[0])
        logits += dot_nt(low_ref[1], high_ref[0])
        mine = (dp * 4 + mp) * rows
        line = lax.broadcasted_iota(jnp.int32, (rows, rows), 0) + mine
        sign = jnp.where(line == mate_buf[...].reshape(1, rows), jnp.float32(1.0), jnp.float32(-1.0))
        coef = -sign * jax.nn.sigmoid(-sign * (scale * logits + offset)) * share
        for kind, tile in ((1, coef), (0, coef.T)):
            high, low = split(tile)
            total = dot(high, high_ref[1 - kind])
            total += dot(high, low_ref[1 - kind])
            total += dot(low, high_ref[1 - kind])
            out_ref[kind] += total

    def multiply(one, other, kind, index):
        lines = pl.ds(pl.multiple_of(index * 2 * piece, 2 * piece), 2 * piece)
        block = jnp.concatenate([buf[one, lines], buf[other, lines]], axis=0)
        high, low = split(block)
        both = jnp.concatenate([high, low], axis=0)
        twice = dot_nt(high_ref[kind], both)
        logits = twice[:, : 4 * piece] + twice[:, 4 * piece :] + dot_nt(low_ref[kind], high)
        coef = jax.nn.sigmoid(scale * logits + offset) * share
        coef_high, coef_low = split(coef)
        out_ref[kind] += dot(
            jnp.concatenate([coef_high, coef_low, coef_high], axis=1),
            jnp.concatenate([high, high, low], axis=0),
        )

    def step(i, carry):
        issue(i + AHEAD)

        @pl.when(i < PIECES)
        def _():
            flows[6](i).start()

        @pl.when(is_outer & (i >= 1) & (i < last))
        def _():
            relay(i)

        @pl.when(is_outer & (i == last))
        def _():
            relay_last()

        @pl.when((x_lo != side) & (i == DETOUR_AT))
        def _():
            out_way.start()

        @pl.when((x_lo != side) & (i == DETOUR_AT + 3))
        def _():
            out_way.wait_recv()
            in_way.start()

        @pl.when(is_outer & (i == TRAIL))
        def _():
            pl.semaphore_wait(barrier, 2)

        @pl.when(is_outer & (i >= TRAIL) & (i < PIECES + TRAIL))
        def _():
            flows[1](i - TRAIL).start()
            flows[3](i - TRAIL).start()

        @pl.when(is_outer & (i >= EARLY_AT) & (i < EARLY_AT + EARLY))
        def _():
            arrived(PASS_Q, i - EARLY_AT)
            flows[4](i - EARLY_AT).start()

        item = i - 2 - lag

        @pl.when((item >= 0) & (item < 2 * PIECES))
        def _():
            half = item // PIECES
            index = (item - half * PIECES) // 2
            spare = jnp.where((core == side) == (half == 0), X4S, SIB)
            first = item % 2 == 0
            one = jnp.where(half == 0, jnp.where(first, A2, A4), jnp.where(first, B2, B4))
            other = jnp.where(first, jnp.where(half == 0, A2S, B2S), spare)
            kind = jnp.where(
                first, jnp.where(half == 0, type_a2, type_b2), jnp.where(half == 0, near, far)
            )
            arrived(other, 2 * index)
            arrived(other, 2 * index + 1)
            multiply(one, other, kind, index)

        late = i - lag

        @pl.when((late >= 0) & (late < PIECES))
        def _():
            arrived(A2, late)
            flows[7](late).start()
            arrived(A4, late)

            @pl.when(core != side)
            def _():
                flows[9](late).start()

        @pl.when((late >= PIECES) & (late < 2 * PIECES))
        def _():
            index = late - PIECES
            arrived(B2, index)
            flows[8](index).start()
            arrived(B4, index)

            @pl.when(core == side)
            def _():
                flows[9](index).start()

        @pl.when(i == PIECES + 1)
        def _():
            diagonal()

        return carry

    lax.fori_loop(0, 2 * PIECES + LAG_OUTER + 2, step, 0)

    def finish(i, carry):
        for flow in (0, 1, 4, 5, 6, 7, 8, 9):
            flows[flow](i).wait_send()

        @pl.when(is_outer)
        def _():
            flows[3](i).wait_send()

        @pl.when(is_outer & (i < last))
        def _():
            flows[2](i).wait_send()

        return carry

    lax.fori_loop(0, PIECES, finish, 0)

    @pl.when(is_outer)
    def _():
        straight.wait_send()

    @pl.when(x_lo != side)
    def _():
        out_way.wait_send()
        in_way.wait_send()


def body(photo_embedding_matrix, caption_embedding_matrix, caption_mate_entry, sharpness_factor, affinity_offset):
    rows, width = photo_embedding_matrix.shape
    planes = lax.axis_size("dp") // 2
    both = pl.pallas_call(
        functools.partial(kernel, planes),
        out_shape=pltpu.VMEM((2, rows, width), jnp.float32),
        in_specs=[
            pl.BlockSpec(memory_space=pltpu.HBM),
            pl.BlockSpec(memory_space=pltpu.HBM),
            pl.BlockSpec(memory_space=pltpu.HBM),
            pl.BlockSpec(memory_space=pltpu.SMEM),
            pl.BlockSpec(memory_space=pltpu.SMEM),
        ],
        out_specs=pl.BlockSpec(memory_space=pltpu.VMEM),
        scratch_shapes=[
            pltpu.VMEM((SLOTS, rows, width), jnp.float32),
            pltpu.VMEM((2, rows, width), jnp.bfloat16),
            pltpu.VMEM((2, rows, width), jnp.bfloat16),
            pltpu.VMEM((rows,), jnp.int32),
            pltpu.SemaphoreType.DMA((10, PIECES)),
            pltpu.SemaphoreType.DMA((SLOTS, PIECES)),
            pltpu.SemaphoreType.DMA((3,)),
            pltpu.SemaphoreType.DMA((PIECES * SLIVERS,)),
            pltpu.SemaphoreType.REGULAR,
        ],
        compiler_params=pltpu.CompilerParams(
            collective_id=0, has_side_effects=True, vmem_limit_bytes=48 * 1024 * 1024
        ),
        cost_estimate=pl.CostEstimate(
            flops=57 * 2 * rows * rows * width,
            bytes_accessed=16 * rows * width,
            transcendentals=9 * rows * rows,
        ),
    )(
        pltpu.with_memory_space_constraint(caption_embedding_matrix, pltpu.HBM),
        pltpu.with_memory_space_constraint(photo_embedding_matrix, pltpu.HBM),
        pltpu.with_memory_space_constraint(caption_mate_entry, pltpu.HBM),
        sharpness_factor,
        affinity_offset,
    )
    return both[0], both[1]


def solution(mesh):
    in_specs = (P(("dp", "mp"), None), P(("dp", "mp"), None), P(("dp", "mp")), P(), P())
    out_specs = (P(("dp", "mp"), None), P(("dp", "mp"), None))
    return jax.shard_map(body, mesh=mesh, in_specs=in_specs, out_specs=out_specs, check_vma=False)
```

```python
import functools

import jax
import jax.numpy as jnp
from jax import lax
from jax.experimental import pallas as pl
from jax.experimental.pallas import tpu as pltpu
from jax.sharding import PartitionSpec as P

HOPS = 4
PIECES = 12
AHEAD = 2
LAG_INNER = 2
LAG_OUTER = 4
TRAIL = 0
SLIVERS = 2
EARLY = 1
EARLY_AT = 6
DETOUR = 3
DETOUR_AT = 7
TEXT, IMAGE, SIB, A2, A4, B2, B4, A2S, B2S, X4S, PASS_P, PASS_Q = range(12)
SLOTS = 12
NT = (((1,), (1,)), ((), ()))


def split(value):
    high = value.astype(jnp.bfloat16)
    return high, (value - high.astype(jnp.float32)).astype(jnp.bfloat16)


def dot(left, right):
    return jnp.dot(left, right, preferred_element_type=jnp.float32)


def dot_nt(left, right):
    return lax.dot_general(left, right, NT, preferred_element_type=jnp.float32)


def kernel(
    planes, text_ref, image_ref, mate_ref, scale_ref, offset_ref, out_ref,
    buf, high_ref, low_ref, mate_buf, send_sem, recv_sem, load_sem, sliver_sem, go_sem,
):
    rows = text_ref.shape[0]
    piece = rows // PIECES
    dp, mp = lax.axis_index("dp"), lax.axis_index("mp")
    plane, x_lo = dp // 2, dp % 2
    side, core = mp // 2, mp % 2
    is_outer = x_lo == side
    lag = jnp.where(is_outer, LAG_OUTER, LAG_INNER)
    near, far = side, 1 - side
    type_a2 = jnp.where(is_outer, far, near)
    type_b2 = jnp.where(is_outer, near, far)

    def at(z, lo, hi, c):
        return (z * 2 + lo, hi * 2 + c)

    beside = at(plane, 1 - x_lo, side, core)
    across = at(plane, 1 - x_lo, 1 - side, core)
    sibling = at(plane, x_lo, side, 1 - core)
    up = at((plane + 1) % planes, x_lo, side, core)
    down = at((plane + planes - 1) % planes, x_lo, side, core)

    def pick(flag, yes, no):
        return tuple(jnp.where(flag, a, b) for a, b in zip(yes, no))

    z_near = pick(side == 0, up, down)
    z_far = pick(side == 0, down, up)

    def move(flow, source, target, index, device):
        lines = pl.ds(pl.multiple_of(index * piece, piece), piece)
        return pltpu.make_async_remote_copy(
            src_ref=buf.at[source, lines],
            dst_ref=buf.at[target, lines],
            send_sem=send_sem.at[flow, index],
            recv_sem=recv_sem.at[target, index],
            device_id=device,
            device_id_type=pl.DeviceIdType.MESH,
        )

    def arrived(slot, index):
        move(0, slot, slot, index, sibling).wait_recv()

    first_target = jnp.where(is_outer, A4, PASS_P)
    second_target = jnp.where(is_outer, PASS_Q, A2)
    second_device = pick(is_outer, z_far, across)
    third_source = jnp.where(is_outer, PASS_Q, A4)
    fourth_source = jnp.where(is_outer, PASS_Q, far)

    flows = [
        lambda i: move(0, near, first_target, i, beside),
        lambda i: move(1, far, second_target, i, second_device),
        lambda i: move(2, PASS_P, A2, i, across),
        lambda i: move(3, PASS_P, A4, i, z_near),
        lambda i: move(4, third_source, B2, i, across),
        lambda i: move(5, fourth_source, B4, i, beside),
        lambda i: move(6, core, SIB, i, sibling),
        lambda i: move(7, A2, A2S, i, sibling),
        lambda i: move(8, B2, B2S, i, sibling),
        lambda i: move(9, jnp.where(core == side, B4, A4), X4S, i, sibling),
    ]

    load_text = pltpu.make_async_copy(text_ref, buf.at[TEXT], load_sem.at[0])
    load_image = pltpu.make_async_copy(image_ref, buf.at[IMAGE], load_sem.at[1])
    load_mate = pltpu.make_async_copy(mate_ref, mate_buf, load_sem.at[2])
    load_text.start()
    load_image.start()
    load_mate.start()

    barrier = pltpu.get_barrier_semaphore()

    def signal(semaphore, device):
        pl.semaphore_signal(semaphore, inc=1, device_id=device, device_id_type=pl.DeviceIdType.MESH)

    @pl.when(is_outer)
    def _():
        signal(barrier, beside)
        signal(barrier, at(plane, 1 - x_lo, side, 1 - core))
        signal(barrier, at(plane, x_lo, 1 - side, core))
        signal(barrier, up)
        signal(barrier, down)

    @pl.when(x_lo != side)
    def _():
        signal(barrier, across)
        signal(barrier, sibling)
        pl.semaphore_wait(barrier, 5)
        signal(go_sem, beside)

    @pl.when(is_outer)
    def _():
        pl.semaphore_wait(go_sem, 1)

    def begin(ref, flow, target, index, device):
        lines = pl.ds(index * piece, piece)
        pltpu.make_async_remote_copy(
            src_ref=ref.at[lines],
            dst_ref=buf.at[target, lines],
            send_sem=send_sem.at[flow, index],
            recv_sem=recv_sem.at[target, index],
            device_id=device,
            device_id_type=pl.DeviceIdType.MESH,
        ).start()

    thin = piece // SLIVERS

    def sliver(ref, flow, target, index, part, recv, device):
        lines = pl.ds(pl.multiple_of(index * piece + part * thin, thin), thin)
        return pltpu.make_async_remote_copy(
            src_ref=ref.at[lines],
            dst_ref=buf.at[target, lines],
            send_sem=send_sem.at[flow, index],
            recv_sem=recv,
            device_id=device,
            device_id_type=pl.DeviceIdType.MESH,
        )

    def begin_slivers(ref, index):
        for part in range(SLIVERS):
            sliver(ref, 0, PASS_P, index, part, sliver_sem.at[index * SLIVERS + part], beside).start()

    last = PIECES - 1
    kept = piece - piece * DETOUR // 4

    def detour(source, flow, target, recv, device):
        lines = pl.ds(last * piece + kept, piece - kept)
        return pltpu.make_async_remote_copy(
            src_ref=buf.at[source, lines],
            dst_ref=buf.at[target, lines],
            send_sem=send_sem.at[flow, last],
            recv_sem=recv,
            device_id=device,
            device_id_type=pl.DeviceIdType.MESH,
        )

    out_way = detour(near, 2, PASS_P, recv_sem.at[PASS_P, last], across)
    in_way = detour(PASS_P, 3, A2, recv_sem.at[A2, last], beside)
    lines_kept = pl.ds(last * piece, kept)
    straight = pltpu.make_async_remote_copy(
        src_ref=buf.at[PASS_P, lines_kept],
        dst_ref=buf.at[A2, lines_kept],
        send_sem=send_sem.at[2, last],
        recv_sem=recv_sem.at[A2, last],
        device_id=across,
        device_id_type=pl.DeviceIdType.MESH,
    )

    def relay_last():
        for part in range(SLIVERS):
            recv = sliver_sem.at[last * SLIVERS + part]
            sliver(buf.at[PASS_P], 2, PASS_P, last, part, recv, across).wait_recv()
        straight.start()

    def relay(index):
        for part in range(SLIVERS):
            source = buf.at[PASS_P]
            sliver(source, 2, PASS_P, index, part, sliver_sem.at[index * SLIVERS + part], across).wait_recv()
            sliver(source, 2, A2, index, part, recv_sem.at[A2, index], across).start()

    for which, near_ref, far_ref in ((0, text_ref, image_ref), (1, image_ref, text_ref)):

        @pl.when((side == which) & is_outer)
        def _(near_ref=near_ref):
            for index in range(AHEAD):
                begin(near_ref, 0, A4, index, beside)

        @pl.when((side == which) & (x_lo != side))
        def _(near_ref=near_ref, far_ref=far_ref):
            for index in range(AHEAD):
                begin_slivers(near_ref, index)
                begin(far_ref, 1, A2, index, across)

    out_ref[...] = jnp.zeros_like(out_ref)

    @pl.when(is_outer)
    def _():
        relay(0)

    load_text.wait()
    load_image.wait()
    load_mate.wait()

    def issue(step):
        @pl.when((step < PIECES) & is_outer)
        def _():
            flows[0](step).start()

        @pl.when((step < PIECES) & (x_lo != side))
        def _():
            begin_slivers(buf.at[near], step)
            flows[1](step).start()

        @pl.when((step >= PIECES) & (step < 2 * PIECES))
        def _():
            index = step - PIECES

            @pl.when(is_outer & (index >= EARLY))
            def _():
                arrived(PASS_Q, index)

            @pl.when((x_lo != side) | (index >= EARLY))
            def _():
                flows[4](index).start()

            flows[5](index).start()

    scale = scale_ref[0]
    offset = offset_ref[0]
    share = scale * jnp.float32(1.0 / (HOPS + 1))

    for kind, slot in ((0, IMAGE), (1, TEXT)):
        high, low = split(buf[slot])
        high_ref[kind] = high
        low_ref[kind] = low

    def diagonal():
        logits = dot_nt(high_ref[1], high_ref[0])
        logits += dot_nt(high_ref[1], low_ref[0])
        logits += dot_nt(low_ref[1], high_ref[0])
        mine = (dp * 4 + mp) * rows
        line = lax.broadcasted_iota(jnp.int32, (rows, rows), 0) + mine
        sign = jnp.where(line == mate_buf[...].reshape(1, rows), jnp.float32(1.0), jnp.float32(-1.0))
        coef = -sign * jax.nn.sigmoid(-sign * (scale * logits + offset)) * share
        for kind, tile in ((1, coef), (0, coef.T)):
            high, low = split(tile)
            total = dot(high, high_ref[1 - kind])
            total += dot(high, low_ref[1 - kind])
            total += dot(low, high_ref[1 - kind])
            out_ref[kind] += total

    def multiply(one, other, kind, index):
        lines = pl.ds(pl.multiple_of(index * 2 * piece, 2 * piece), 2 * piece)
        block = jnp.concatenate([buf[one, lines], buf[other, lines]], axis=0)
        high, low = split(block)
        both = jnp.concatenate([high, low], axis=0)
        twice = dot_nt(high_ref[kind], both)
        logits = twice[:, : 4 * piece] + twice[:, 4 * piece :] + dot_nt(low_ref[kind], high)
        coef = jax.nn.sigmoid(scale * logits + offset) * share
        coef_high, coef_low = split(coef)
        out_ref[kind] += dot(
            jnp.concatenate([coef_high, coef_low, coef_high], axis=1),
            jnp.concatenate([high, high, low], axis=0),
        )

    def step(i, carry):
        issue(i + AHEAD)

        @pl.when(i < PIECES)
        def _():
            flows[6](i).start()

        @pl.when(is_outer & (i >= 1) & (i < last))
        def _():
            relay(i)

        @pl.when(is_outer & (i == last))
        def _():
            relay_last()

        @pl.when((x_lo != side) & (i == DETOUR_AT))
        def _():
            out_way.start()

        @pl.when((x_lo != side) & (i == DETOUR_AT + 3))
        def _():
            out_way.wait_recv()
            in_way.start()

        @pl.when(is_outer & (i == TRAIL))
        def _():
            pl.semaphore_wait(barrier, 2)

        @pl.when(is_outer & (i >= TRAIL) & (i < PIECES + TRAIL))
        def _():
            flows[1](i - TRAIL).start()
            flows[3](i - TRAIL).start()

        @pl.when(is_outer & (i >= EARLY_AT) & (i < EARLY_AT + EARLY))
        def _():
            arrived(PASS_Q, i - EARLY_AT)
            flows[4](i - EARLY_AT).start()

        item = i - 2 - lag

        @pl.when((item >= 0) & (item < 2 * PIECES))
        def _():
            half = item // PIECES
            index = (item - half * PIECES) // 2
            spare = jnp.where((core == side) == (half == 0), X4S, SIB)
            first = (item % 2 == 0) != ((half == 1) & (core == side))
            one = jnp.where(half == 0, jnp.where(first, A2, A4), jnp.where(first, B2, B4))
            other = jnp.where(first, jnp.where(half == 0, A2S, B2S), spare)
            kind = jnp.where(
                first, jnp.where(half == 0, type_a2, type_b2), jnp.where(half == 0, near, far)
            )
            arrived(other, 2 * index)
            arrived(other, 2 * index + 1)
            multiply(one, other, kind, index)

        late = i - lag

        @pl.when((late >= 0) & (late < PIECES))
        def _():
            arrived(A2, late)
            flows[7](late).start()
            arrived(A4, late)

            @pl.when(core != side)
            def _():
                flows[9](late).start()

        @pl.when((late >= PIECES) & (late < 2 * PIECES))
        def _():
            index = late - PIECES
            arrived(B2, index)
            flows[8](index).start()
            arrived(B4, index)

            @pl.when(core == side)
            def _():
                flows[9](index).start()

        @pl.when(i == PIECES + 1)
        def _():
            diagonal()

        return carry

    lax.fori_loop(0, 2 * PIECES + LAG_OUTER + 2, step, 0)

    def finish(i, carry):
        for flow in (0, 1, 4, 5, 6, 7, 8, 9):
            flows[flow](i).wait_send()

        @pl.when(is_outer)
        def _():
            flows[3](i).wait_send()

        @pl.when(is_outer & (i < last))
        def _():
            flows[2](i).wait_send()

        return carry

    lax.fori_loop(0, PIECES, finish, 0)

    @pl.when(is_outer)
    def _():
        straight.wait_send()

    @pl.when(x_lo != side)
    def _():
        out_way.wait_send()
        in_way.wait_send()


def body(photo_embedding_matrix, caption_embedding_matrix, caption_mate_entry, sharpness_factor, affinity_offset):
    rows, width = photo_embedding_matrix.shape
    planes = lax.axis_size("dp") // 2
    both = pl.pallas_call(
        functools.partial(kernel, planes),
        out_shape=pltpu.VMEM((2, rows, width), jnp.float32),
        in_specs=[
            pl.BlockSpec(memory_space=pltpu.HBM),
            pl.BlockSpec(memory_space=pltpu.HBM),
            pl.BlockSpec(memory_space=pltpu.HBM),
            pl.BlockSpec(memory_space=pltpu.SMEM),
            pl.BlockSpec(memory_space=pltpu.SMEM),
        ],
        out_specs=pl.BlockSpec(memory_space=pltpu.VMEM),
        scratch_shapes=[
            pltpu.VMEM((SLOTS, rows, width), jnp.float32),
            pltpu.VMEM((2, rows, width), jnp.bfloat16),
            pltpu.VMEM((2, rows, width), jnp.bfloat16),
            pltpu.VMEM((rows,), jnp.int32),
            pltpu.SemaphoreType.DMA((10, PIECES)),
            pltpu.SemaphoreType.DMA((SLOTS, PIECES)),
            pltpu.SemaphoreType.DMA((3,)),
            pltpu.SemaphoreType.DMA((PIECES * SLIVERS,)),
            pltpu.SemaphoreType.REGULAR,
        ],
        compiler_params=pltpu.CompilerParams(
            collective_id=0, has_side_effects=True, vmem_limit_bytes=48 * 1024 * 1024
        ),
        cost_estimate=pl.CostEstimate(
            flops=57 * 2 * rows * rows * width,
            bytes_accessed=16 * rows * width,
            transcendentals=9 * rows * rows,
        ),
    )(
        pltpu.with_memory_space_constraint(caption_embedding_matrix, pltpu.HBM),
        pltpu.with_memory_space_constraint(photo_embedding_matrix, pltpu.HBM),
        pltpu.with_memory_space_constraint(caption_mate_entry, pltpu.HBM),
        sharpness_factor,
        affinity_offset,
    )
    return both[0], both[1]


def solution(mesh):
    in_specs = (P(("dp", "mp"), None), P(("dp", "mp"), None), P(("dp", "mp")), P(), P())
    out_specs = (P(("dp", "mp"), None), P(("dp", "mp"), None))
    return jax.shard_map(body, mesh=mesh, in_specs=in_specs, out_specs=out_specs, check_vma=False)
```
